512 devices in a mesh: group: 32 (over z_lo, x), fsdp: 16 (over y, z_hi, core).
Axes of the slice: x: 4, y: 4, z: 16 (z_hi: 2, z_lo: 8; z = z_hi * 8 + z_lo), core: 2. Of those that a mesh axis runs over, the one named last changes fastest.
Arguments:
- tokens: bfloat16 [32, 2048, 2304], P('group', 'fsdp'), may hold values from -6 to 6
- token_ids: int32 [32, 2048], P('group', 'fsdp'), may hold values from 0 to 255999
- weight: bfloat16 [32, 2304, 1024], P('group', 'fsdp'), may hold values from -0.125 to 0.125
- stale_weight: bfloat16 [32, 2304, 1024], P('group', 'fsdp'), may hold values from -0.125 to 0.125
- gain: bfloat16 [32, 2304], P('group'), may hold values from 0.099609375 to 1.8984375
- stale_gain: bfloat16 [32, 2304], P('group'), may hold values from 0.099609375 to 1.8984375
- partner: int32 [32], replicated, may hold values from 0 to 31, as said below
Outputs:
- grad_weight: float32 [32, 2304, 1024], P('group', 'fsdp')
- grad_tokens: bfloat16 [32, 2048, 2304], P('group', 'fsdp')
- token_loss: float32 [32, 2048], P('group', 'fsdp')
The draws below stay inside these ranges and needn't reach their ends.
Inputs may be any that keep to these rules, and one draw needn't show every extreme that they name: partner[g] = g XOR m for one m of 1 to 31, the same for all g.
All inputs are finite; a program needn't handle non-finite values.
Results may differ from the reference program's by a relative error of at most 0.01.
Values may be sent and summed in bfloat16 or wider, within the bound.
A program may use at most 64 MiB of HBM per device.

```python
import jax
import jax.numpy as jnp
from jax import lax

D = 2304
F = 1024
VOCAB = 256000
GTOK = 2048
NGROUPS = 32


def draw_partner(key, part):
    key = jax.random.fold_in(key, 11)
    flip = jax.random.randint(key, (), 1, NGROUPS, dtype=jnp.int32)
    return jnp.bitwise_xor(jnp.arange(NGROUPS, dtype=jnp.int32), flip)


def draw_token_ids(key, part):
    key = jax.random.fold_in(key, 23)
    first, second = jax.random.split(key)
    values = jax.random.randint(first, (NGROUPS, GTOK), 1, VOCAB, dtype=jnp.int32)
    padded = jax.random.randint(second, (NGROUPS, GTOK), 0, 4, dtype=jnp.int32)
    return jnp.where(padded == 0, jnp.int32(0), values)


def block_levels(key, extent, shards, least, top_value):
    level, own = 1.0, jax.random.fold_in(key, 6)
    for axis_at, shards_of in shards:
        steps = jnp.exp(jax.random.uniform(jax.random.fold_in(own, axis_at), (shards_of,), jnp.float32, least / len(shards), top_value / len(shards)))
        level = level * jnp.repeat(steps, extent[axis_at] // shards_of).reshape([-1 if axis == axis_at else 1 for axis in range(len(extent))])
    return level


def noise(key, dims, scale, limit, cuts=(), kind=jnp.bfloat16):
    factor_of = block_levels(key, dims, cuts, -0.22, 0.18) if cuts else 1.0
    values = jax.random.normal(key, dims, jnp.float32) * scale * factor_of
    return jnp.minimum(jnp.maximum(values, -limit), limit).astype(kind)


def setup_inputs(seed: int = 0) -> dict:
    key_list = jax.random.split(jax.random.key(seed), 8)
    tokens = noise(key_list[0], (NGROUPS, GTOK, D), 1.0, 6.0, ((0, 32), (1, 16)))
    token_ids = draw_token_ids(jax.random.fold_in(key_list[7], 71), 0)
    weight = noise(key_list[2], (NGROUPS, D, F), D ** -0.5, 0.125, ((0, 32), (1, 16)))
    stale_weight = noise(key_list[3], (NGROUPS, D, F), D ** -0.5, 0.125, ((0, 32), (1, 16)))
    gain = jnp.clip(1.0 + 0.18 * jax.random.normal(key_list[4], (NGROUPS, D), jnp.float32), 0.099609375, 1.8984375).astype(jnp.bfloat16)
    stale_gain = jnp.clip(1.0 + 0.18 * jax.random.normal(key_list[5], (NGROUPS, D), jnp.float32), 0.099609375, 1.8984375).astype(jnp.bfloat16)
    partner = draw_partner(jax.random.fold_in(key_list[7], 71), 0)
    return {"tokens": tokens, "token_ids": token_ids, "weight": weight, "stale_weight": stale_weight, "gain": gain, "stale_gain": stale_gain, "partner": partner}


def one_group(args):
    xin, ids, wcur, gcur, wold, gold = args
    x = xin.astype(jnp.float32)
    rstd = lax.rsqrt(lax.optimization_barrier(jnp.mean(x * x, axis=-1, keepdims=True)) + 1e-06)
    normed = x * rstd
    student_in = (normed * gcur.astype(jnp.float32)).astype(jnp.bfloat16)
    teacher_in = (normed * gold.astype(jnp.float32)).astype(jnp.bfloat16)
    student_out = jnp.dot(student_in, wcur, preferred_element_type=jnp.float32)
    teacher_out = jnp.dot(teacher_in, wold, preferred_element_type=jnp.float32)
    keep = (ids != 0).astype(jnp.float32)[:, None]
    diff = keep * (student_out - teacher_out)
    loss = 0.5 * lax.optimization_barrier(jnp.mean(diff * diff, axis=-1))
    out_grad = diff.astype(jnp.bfloat16)
    grad_w = lax.dot_general(student_in, out_grad, (((0,), (0,)), ((), ())), preferred_element_type=jnp.float32)
    grad_w = grad_w / jnp.sqrt(jnp.float32(GTOK))
    in_grad = lax.dot_general(out_grad, wcur, (((1,), (1,)), ((), ())), preferred_element_type=jnp.float32)
    scaled = in_grad * gcur.astype(jnp.float32)
    grad_x = rstd * (scaled - normed * lax.optimization_barrier(jnp.mean(scaled * normed, axis=-1, keepdims=True)))
    return (grad_w, grad_x.astype(jnp.bfloat16), loss)

def reference(tokens, token_ids, weight, stale_weight, gain, stale_gain, partner):
    mates = partner.astype(jnp.int32)
    wold = stale_weight[mates]
    gold = stale_gain[mates]
    grad_weight, grad_tokens, token_loss = lax.map(one_group, (tokens, token_ids, weight, gain, wold, gold))
    return (grad_weight, grad_tokens, token_loss)
```

```python
import functools

import jax
import jax.numpy as jnp
from jax import lax
from jax.experimental import pallas as pl
from jax.experimental.pallas import tpu as pltpu
from jax.sharding import PartitionSpec as P

MESH = pl.DeviceIdType.MESH
NY = 4
CHUNKS = 4
F32 = jnp.float32
BF16 = jnp.bfloat16


def step_kernel(
    x_ref, keep_ref, w_ref, sa_ref, sb_ref, gain_ref, sgain_ref,
    gw_ref, gt_ref, loss_ref,
    x4, xc, xt, wfull, sfull, gcol, sgcol, grow,
    pself, psend, precv, og, igacc, igsend, igrecv,
    gmsend, gmrecv, gzkeep, gzsend, gzrecv, rstd_ref,
    ysend, yrecv, csend, crecv, zsend, zrecv,
):
    tok, dim = x_ref.shape
    rows, feat = w_ref.shape
    chans = dim // NY
    width = feat // CHUNKS
    grp = lax.axis_index("group")
    me = lax.axis_index("fsdp")
    y = me // 4
    zc = lax.rem(me, 4)
    zh = zc // 2
    core = lax.rem(zc, 2)
    mate = (grp, y * 4 + zh * 2 + (1 - core))
    twin = (grp, y * 4 + (1 - zh) * 2 + core)

    def at_y(k):
        return (grp, lax.rem(y + k, NY) * 4 + zc)

    def remote(src, dst, ss, rs, dev):
        return pltpu.make_async_remote_copy(
            src_ref=src, dst_ref=dst, send_sem=ss, recv_sem=rs,
            device_id=dev, device_id_type=MESH,
        )

    def block(b):
        return pl.ds(pl.multiple_of(b * rows, 16), rows)

    sent = []

    def go(copy):
        copy.start()
        sent.append(copy)

    barrier = pltpu.get_barrier_semaphore()
    for peer in [mate, twin] + [at_y(k) for k in range(1, NY)]:
        pl.semaphore_signal(barrier, inc=1, device_id=peer, device_id_type=MESH)

    for q in range(NY):
        x4[q] = x_ref[:, q * chans:(q + 1) * chans]
    mine = zc
    wfull[block(mine), :] = w_ref[...]
    pl.semaphore_wait(barrier, NY + 1)

    cols = [pl.ds(f * width, width) for f in range(CHUNKS)]
    for f in range(CHUNKS):
        go(remote(w_ref.at[:, cols[f]], wfull.at[block(mine), cols[f]],
                  zsend.at[f], zrecv.at[f], twin))
    far = (1 - zh) * 2 + core
    go(remote(w_ref, wfull.at[block(mine), :], csend.at[0], crecv.at[0], mate))
    go(remote(sa_ref, sfull.at[block(mine), :], csend.at[1], crecv.at[1], mate))
    go(remote(sb_ref, sfull.at[block(far), :], csend.at[2], crecv.at[2], mate))
    for k in range(1, NY):
        go(remote(x4.at[lax.rem(y + k, NY)], xc.at[k], ysend.at[0, k], yrecv.at[0, k], at_y(k)))
    xc[0] = x4[y]
    sfull[block(mine), :] = sa_ref[...]
    sfull[block(far), :] = sb_ref[...]

    xf = x_ref[...].astype(F32)
    rstd_ref[...] = lax.rsqrt(jnp.mean(xf * xf, axis=1, keepdims=True) + 1e-06)
    for q in range(NY):
        grow[q] = gain_ref[:, q * chans:(q + 1) * chans].astype(F32)

    gcol[...] = jnp.broadcast_to(grow[y], (128, chans)).T
    sgcol[...] = jnp.broadcast_to(sgain_ref[...].astype(F32), (128, chans)).T

    def y_wait(n, k, ref):
        remote(ref, ref, ysend.at[n, k], yrecv.at[n, k], at_y(k)).wait_recv()

    def c_wait(n, ref):
        remote(ref, ref, csend.at[n], crecv.at[n], mate).wait_recv()

    def z_wait(n, ref):
        remote(ref, ref, zsend.at[n], zrecv.at[n], twin).wait_recv()

    for k in range(1, NY):
        y_wait(0, k, xc.at[k])
    for k in range(NY):
        xt[:, k * tok:(k + 1) * tok] = xc[k].T
    other = zh * 2 + (1 - core)
    otherfar = (1 - zh) * 2 + (1 - core)
    c_wait(0, wfull.at[block(other), :])
    c_wait(1, sfull.at[block(other), :])
    c_wait(2, sfull.at[block(otherfar), :])

    igacc[...] = jnp.zeros_like(igacc)
    gcolv = gcol[:, 0:1]
    sgcolv = sgcol[:, 0:1]

    def stage_a(f):
        z_wait(f, wfull.at[block(far), cols[f]])
        go(remote(wfull.at[block(far), cols[f]], wfull.at[block(far), cols[f]],
                  csend.at[3 + f], crecv.at[3 + f], mate))
        c_wait(3 + f, wfull.at[block(otherfar), cols[f]])
        c = (gcolv * wfull[:, cols[f]].astype(F32) - sgcolv * sfull[:, cols[f]].astype(F32)).astype(BF16)
        for k in [1, 3, 2, 0]:
            part = jnp.dot(xc[k], c, preferred_element_type=F32)
            if k == 0:
                pself[f] = part
            else:
                back = NY - k
                psend[f, k] = part.astype(BF16)
                go(remote(psend.at[f, k], precv.at[f, back],
                          ysend.at[1 + f, back], yrecv.at[1 + f, back], at_y(back)))

    def stage_b(f):
        total = pself[f]
        for k in range(1, NY):
            y_wait(1 + f, k, precv.at[f, k])
            total = total + precv[f, k].astype(F32)
        rstd = rstd_ref[...]
        diff = total * (rstd * keep_ref[...])
        og[f, 0] = (diff * rstd).astype(BF16)
        for k in range(1, NY):
            go(remote(og.at[f, 0], og.at[f, k],
                      ysend.at[1 + CHUNKS + f, k], yrecv.at[1 + CHUNKS + f, k], at_y(k)))
        return jnp.sum(diff * diff, axis=1, keepdims=True)

    def stage_c(f):
        for k in range(1, NY):
            y_wait(1 + CHUNKS + f, k, og.at[f, k])
        ogf = og[f].reshape(NY * tok, width)
        g = jnp.dot(xt[...], ogf, preferred_element_type=F32)
        pself_gw = g
        gfull = gmsend.at[f]
        gfull[...] = pself_gw
        for n, b in enumerate([otherfar, other]):
            go(remote(gfull.at[block(b), :], gmrecv.at[f, n],
                      csend.at[3 + CHUNKS + 2 * f + n], crecv.at[3 + CHUNKS + 2 * f + n], mate))
        igacc[...] += lax.dot_general(ogf, wfull[:, cols[f]], (((1,), (1,)), ((), ())),
                                      preferred_element_type=F32)

    def stage_d(f):
        c_wait(3 + CHUNKS + 2 * f, gmrecv.at[f, 0])
        gzsend[f] = (gmsend[f, block(far), :] + gmrecv[f, 0]).astype(BF16)
        go(remote(gzsend.at[f], gzrecv.at[f], zsend.at[CHUNKS + f], zrecv.at[CHUNKS + f], twin))
        c_wait(3 + CHUNKS + 2 * f + 1, gmrecv.at[f, 1])
        gzkeep[f] = gmsend[f, block(mine), :] + gmrecv[f, 1]

    loss = jnp.zeros((tok, 1), F32)
    stage_a(0)
    for f in range(CHUNKS):
        loss = loss + stage_b(f)
        if f >= 1:
            stage_d(f - 1)
        if f + 1 < CHUNKS:
            stage_a(f + 1)
        stage_c(f)
    stage_d(CHUNKS - 1)
    loss_ref[...] = loss * (0.5 / feat)

    last = 1 + 2 * CHUNKS
    for k in range(NY):
        igsend[k] = igacc[k * tok:(k + 1) * tok, :].astype(BF16)
        if k:
            back = NY - k
            go(remote(igsend.at[k], igrecv.at[y],
                      ysend.at[last, back], yrecv.at[last, back], at_y(back)))
    igrecv[y] = igsend[0]
    for k in range(1, NY):
        y_wait(last, k, igrecv.at[lax.rem(y - k + NY, NY)])
    rstd = rstd_ref[...]
    mean = jnp.zeros((tok, 1), F32)
    for q in range(NY):
        scaled = igrecv[q].astype(F32) * grow[q]
        mean = mean + jnp.sum(scaled * x4[q].astype(F32), axis=1, keepdims=True)
    mean = mean * (rstd * (rstd / dim))
    for q in range(NY):
        scaled = igrecv[q].astype(F32) * grow[q]
        gt_ref[:, q * chans:(q + 1) * chans] = (scaled - x4[q].astype(F32) * mean).astype(BF16)

    scale = gcol[block(mine), 0:1] * (1.0 / (16.0 * tok) ** 0.5)
    for f in range(CHUNKS):
        z_wait(CHUNKS + f, gzrecv.at[f])
        gw_ref[:, cols[f]] = (gzkeep[f] + gzrecv[f].astype(F32)) * scale
    for copy in sent:
        copy.wait_send()


def swap_stale(stale, sgain, partner, ngroups, nshard):
    def branch(m):
        def run(s, g):
            same = [(i, i ^ m) for i in range(ngroups)]
            cross = [(i * nshard + d, (i ^ m) * nshard + (d ^ 2))
                     for i in range(ngroups) for d in range(nshard)]
            return (lax.ppermute(s, "group", same),
                    lax.ppermute(s, ("group", "fsdp"), cross),
                    lax.ppermute(g, "group", same))
        return run

    return lax.switch(partner[0] - 1, [branch(m) for m in range(1, ngroups)], stale, sgain)


def body(ngroups, nshard, tokens, token_ids, weight, stale_weight, gain, stale_gain, partner):
    x = tokens[0]
    w = weight[0]
    tok, dim = x.shape
    rows, feat = w.shape
    chans = dim // NY
    width = feat // CHUNKS
    y = lax.axis_index("fsdp") // 4
    sg = lax.dynamic_slice(stale_gain, (0, y * chans), (1, chans))
    sa, sb, sg = swap_stale(stale_weight[0], sg, partner, ngroups, nshard)
    keep = (token_ids[0] != 0).astype(F32)[:, None]
    vm = pl.BlockSpec(memory_space=pltpu.VMEM)
    gw, gt, loss = pl.pallas_call(
        step_kernel,
        out_shape=(
            jax.ShapeDtypeStruct((rows, feat), F32),
            jax.ShapeDtypeStruct((tok, dim), BF16),
            jax.ShapeDtypeStruct((tok, 1), F32),
        ),
        in_specs=[vm] * 7,
        out_specs=(vm, vm, vm),
        scratch_shapes=[
            pltpu.VMEM((NY, tok, chans), BF16),
            pltpu.VMEM((NY, tok, chans), BF16),
            pltpu.VMEM((chans, NY * tok), BF16),
            pltpu.VMEM((chans, feat), BF16),
            pltpu.VMEM((chans, feat), BF16),
            pltpu.VMEM((chans, 128), F32),
            pltpu.VMEM((chans, 128), F32),
            pltpu.VMEM((NY, 1, chans), F32),
            pltpu.VMEM((CHUNKS, tok, width), F32),
            pltpu.VMEM((CHUNKS, NY, tok, width), BF16),
            pltpu.VMEM((CHUNKS, NY, tok, width), BF16),
            pltpu.VMEM((CHUNKS, NY, tok, width), BF16),
            pltpu.VMEM((NY * tok, chans), F32),
            pltpu.VMEM((NY, tok, chans), BF16),
            pltpu.VMEM((NY, tok, chans), BF16),
            pltpu.VMEM((CHUNKS, chans, width), F32),
            pltpu.VMEM((CHUNKS, 2, rows, width), F32),
            pltpu.VMEM((CHUNKS, rows, width), F32),
            pltpu.VMEM((CHUNKS, rows, width), BF16),
            pltpu.VMEM((CHUNKS, rows, width), BF16),
            pltpu.VMEM((tok, 1), F32),
            pltpu.SemaphoreType.DMA((2 + 2 * CHUNKS, NY)),
            pltpu.SemaphoreType.DMA((2 + 2 * CHUNKS, NY)),
            pltpu.SemaphoreType.DMA((3 + 3 * CHUNKS,)),
            pltpu.SemaphoreType.DMA((3 + 3 * CHUNKS,)),
            pltpu.SemaphoreType.DMA((2 * CHUNKS,)),
            pltpu.SemaphoreType.DMA((2 * CHUNKS,)),
        ],
        compiler_params=pltpu.CompilerParams(
            collective_id=0, has_side_effects=True, vmem_limit_bytes=48 * 2**20
        ),
        name="codistill_step",
    )(x, keep, w, sa, sb, gain, sg)
    return gw[None], gt[None], loss[:, 0][None]


def solution(mesh):
    return jax.shard_map(
        functools.partial(body, mesh.shape["group"], mesh.shape["fsdp"]),
        mesh=mesh,
        in_specs=(
            P("group", "fsdp", None),
            P("group", "fsdp"),
            P("group", "fsdp", None),
            P("group", "fsdp", None),
            P("group", None),
            P("group", None),
            P(),
        ),
        out_specs=(P("group", "fsdp", None), P("group", "fsdp", None), P("group", "fsdp")),
        check_vma=False,
    )
```

```python
import functools

import jax
import jax.numpy as jnp
from jax import lax
from jax.experimental import pallas as pl
from jax.experimental.pallas import tpu as pltpu
from jax.sharding import PartitionSpec as P

MESH = pl.DeviceIdType.MESH
NY = 4
CHUNKS = 4
EARLY = 2
F32 = jnp.float32
BF16 = jnp.bfloat16
VM = pl.BlockSpec(memory_space=pltpu.VMEM)


def flip_bits(index, m):
    bit = 1
    while bit <= m:
        if m & bit:
            index = index + bit * (1 - 2 * lax.rem(index // bit, 2))
        bit *= 2
    return index


class Place:
    def __init__(self, rows):
        self.rows = rows
        self.grp = lax.axis_index("group")
        self.me = lax.axis_index("fsdp")
        self.y = self.me // 4
        self.mine = lax.rem(self.me, 4)
        zh = self.mine // 2
        core = lax.rem(self.mine, 2)
        self.far = (1 - zh) * 2 + core
        self.other = zh * 2 + (1 - core)
        self.otherfar = (1 - zh) * 2 + (1 - core)
        self.mate = (self.grp, self.y * 4 + self.other)
        self.twin = (self.grp, self.y * 4 + self.far)

    def at_y(self, k):
        return (self.grp, lax.rem(self.y + k, NY) * 4 + self.mine)

    def block(self, b):
        return pl.ds(pl.multiple_of(b * self.rows, 16), self.rows)

    def greet(self, peers):
        barrier = pltpu.get_barrier_semaphore()
        for peer in peers:
            pl.semaphore_signal(barrier, inc=1, device_id=peer, device_id_type=MESH)
        return lambda: pl.semaphore_wait(barrier, len(peers))


def remote(src, dst, send, recv, dev):
    return pltpu.make_async_remote_copy(
        src_ref=src, dst_ref=dst, send_sem=send, recv_sem=recv,
        device_id=dev, device_id_type=MESH,
    )


def exchange_kernel(
    m,
    x_ref, w_ref, s_ref, sgain_ref,
    xc, wfull, sfull, sgrecv,
    x4, sgrow,
    ysend, yrecv, csend, crecv, zsend, zrecv,
):
    tok, dim = x_ref.shape
    rows, feat = w_ref.shape
    chans = dim // NY
    early = feat * EARLY // CHUNKS
    p = Place(rows)
    partner = flip_bits(p.grp, m)
    near = (partner, p.me)
    cross = (partner, p.y * 4 + p.far)
    peers = [near, cross, p.twin, p.mate] + [p.at_y(k) for k in range(1, NY)]
    arrive = p.greet(peers)
    sent = []

    def go(copy):
        copy.start()
        sent.append(copy)

    for q in range(NY):
        sgrow[q] = sgain_ref[:, q * chans:(q + 1) * chans].astype(F32)

    def cut(i, carry):
        at = pl.ds(pl.multiple_of(i * 16, 16), 16)
        for q in range(NY):
            x4[q, at, :] = x_ref[at, q * chans:(q + 1) * chans]
        return carry

    lax.fori_loop(0, tok // 16, cut, 0)
    arrive()

    mine = p.block(p.mine)
    go(remote(sgrow.at[p.y], sgrecv, zsend.at[3], zrecv.at[3], near))
    go(remote(s_ref, sfull.at[mine, :], zsend.at[0], zrecv.at[0], cross))
    go(remote(s_ref, sfull.at[mine, :], zsend.at[1], zrecv.at[1], near))
    if early:
        go(remote(w_ref.at[:, 0:early], wfull.at[mine, 0:early], zsend.at[2], zrecv.at[2], p.twin))
    go(remote(w_ref, wfull.at[mine, :], csend.at[0], crecv.at[0], p.mate))
    for k in range(1, NY):
        go(remote(x4.at[lax.rem(p.y + k, NY)], xc.at[k], ysend.at[k], yrecv.at[k], p.at_y(k)))
    local = [
        pltpu.make_async_copy(w_ref, wfull.at[mine, :], csend.at[4]),
        pltpu.make_async_copy(x4.at[p.y], xc.at[0], csend.at[5]),
    ]
    for copy in local:
        copy.start()

    far = p.block(p.far)
    arrivals = [(1, sfull.at[mine, :]), (0, sfull.at[far, :])]
    if early:
        arrivals.append((2, wfull.at[far, 0:early]))
    for n, ref in arrivals:
        remote(ref, ref, zsend.at[n], zrecv.at[n], p.twin).wait_recv()
        go(remote(ref, ref, csend.at[1 + n], crecv.at[1 + n], p.mate))

    remote(sgrecv, sgrecv, zsend.at[3], zrecv.at[3], near).wait_recv()
    for k in range(1, NY):
        remote(xc.at[k], xc.at[k], ysend.at[k], yrecv.at[k], p.at_y(k)).wait_recv()
    other = p.block(p.other)
    otherfar = p.block(p.otherfar)
    landed = [(0, wfull.at[other, :]), (2, sfull.at[other, :]), (1, sfull.at[otherfar, :])]
    if early:
        landed.append((3, wfull.at[otherfar, 0:early]))
    for n, ref in landed:
        remote(ref, ref, csend.at[n], crecv.at[n], p.mate).wait_recv()
    for copy in local:
        copy.wait()
    for copy in sent:
        copy.wait_send()


def exchange_for(m, x, w, s, sgain):
    tok, dim = x.shape
    rows, feat = w.shape
    chans = dim // NY
    return pl.pallas_call(
        functools.partial(exchange_kernel, m),
        out_shape=(
            jax.ShapeDtypeStruct((NY, tok, chans), BF16),
            jax.ShapeDtypeStruct((chans, feat), BF16),
            jax.ShapeDtypeStruct((chans, feat), BF16),
            jax.ShapeDtypeStruct((1, chans), F32),
        ),
        in_specs=[VM] * 4,
        out_specs=(VM,) * 4,
        scratch_shapes=[
            pltpu.VMEM((NY, tok, chans), BF16),
            pltpu.VMEM((NY, 1, chans), F32),
            pltpu.SemaphoreType.DMA((NY,)),
            pltpu.SemaphoreType.DMA((NY,)),
            pltpu.SemaphoreType.DMA((6,)),
            pltpu.SemaphoreType.DMA((6,)),
            pltpu.SemaphoreType.DMA((4,)),
            pltpu.SemaphoreType.DMA((4,)),
        ],
        compiler_params=pltpu.CompilerParams(
            collective_id=m, has_side_effects=True, vmem_limit_bytes=16 * 2**20
        ),
        name="exchange",
    )(x, w, s, sgain)


def step_kernel(
    x_ref, ids_ref, w_ref, gain_ref, xc, wfull, sfull, sg_ref,
    gw_ref, gt_ref, loss_ref,
    xt, wlate, cfull, gcol, sgcol, grow,
    pself, psend, precv, og, igacc, igsend, igrecv,
    gmsend, gmrecv, gzkeep, gzsend, gzrecv, rstd_ref, keep_ref,
    ysend, yrecv, csend, crecv, zsend, zrecv,
):
    tok, dim = x_ref.shape
    rows, feat = w_ref.shape
    chans = dim // NY
    width = feat // CHUNKS
    p = Place(rows)
    y = p.y
    arrive = p.greet([p.twin, p.mate] + [p.at_y(k) for k in range(1, NY)])
    sent = []

    def go(copy):
        copy.start()
        sent.append(copy)

    def y_wait(n, k, ref):
        remote(ref, ref, ysend.at[n, k], yrecv.at[n, k], p.at_y(k)).wait_recv()

    def c_wait(n, ref):
        remote(ref, ref, csend.at[n], crecv.at[n], p.mate).wait_recv()

    def z_wait(n, ref):
        remote(ref, ref, zsend.at[n], zrecv.at[n], p.twin).wait_recv()

    block = p.block
    cols = [pl.ds(f * width, width) for f in range(CHUNKS)]

    for q in range(NY):
        grow[q] = gain_ref[:, q * chans:(q + 1) * chans].astype(F32)
    gcol[...] = jnp.broadcast_to(grow[y], (128, chans)).T
    sgcol[...] = jnp.broadcast_to(sg_ref[...], (128, chans)).T

    def weights(f):
        return wfull[:, cols[f]] if f < EARLY else wlate[f - EARLY]

    def stage_a(f):
        if f >= EARLY:
            n = f - EARLY
            z_wait(n, wlate.at[n, block(p.far), :])
            go(remote(wlate.at[n, block(p.far), :], wlate.at[n, block(p.far), :],
                      csend.at[n], crecv.at[n], p.mate))
            for b in (p.mine, p.other):
                wlate[n, block(b), :] = wfull[block(b), cols[f]]
            c_wait(n, wlate.at[n, block(p.otherfar), :])
        c = (gcol[:, 0:1] * weights(f).astype(F32) - sgcol[:, 0:1] * sfull[:, cols[f]].astype(F32))
        cfull[...] = c.astype(BF16)
        for k in [2, 1, 3, 0]:
            part = jnp.dot(xc[k], cfull[...], preferred_element_type=F32)
            if k == 0:
                pself[f] = part
            else:
                back = NY - k
                psend[f, k] = part.astype(BF16)
                if f == 0 and k == 2:
                    arrive()
                    for n in range(CHUNKS - EARLY):
                        go(remote(w_ref.at[:, cols[EARLY + n]], wlate.at[n, block(p.mine), :],
                                  zsend.at[n], zrecv.at[n], p.twin))
                go(remote(psend.at[f, k], precv.at[f, back],
                          ysend.at[f, back], yrecv.at[f, back], p.at_y(back)))

    def stage_b(f):
        total = pself[f]
        for k in range(1, NY):
            y_wait(f, k, precv.at[f, k])
            total = total + precv[f, k].astype(F32)
        rstd = rstd_ref[...]
        diff = total * (rstd * keep_ref[...])
        og[f, 0] = (diff * rstd).astype(BF16)
        for k in [2, 1, 3]:
            go(remote(og.at[f, 0], og.at[f, k],
                      ysend.at[CHUNKS + f, k], yrecv.at[CHUNKS + f, k], p.at_y(k)))
        return jnp.sum(diff * diff, axis=1, keepdims=True)

    def stage_c(f):
        first = CHUNKS + 2 * f
        for k in range(1, NY):
            y_wait(CHUNKS + f, k, og.at[f, k])
        ogf = og[f].reshape(NY * tok, width)
        gmsend[f] = jnp.dot(xt[...], ogf, preferred_element_type=F32)
        for n, b in enumerate([p.otherfar, p.other]):
            go(remote(gmsend.at[f, block(b), :], gmrecv.at[f, n],
                      csend.at[first + n], crecv.at[first + n], p.mate))
        igacc[...] += lax.dot_general(ogf, weights(f), (((1,), (1,)), ((), ())),
                                      preferred_element_type=F32)
        c_wait(first, gmrecv.at[f, 0])
        gzsend[f] = (gmsend[f, block(p.far), :] + gmrecv[f, 0]).astype(BF16)
        go(remote(gzsend.at[f], gzrecv.at[f], zsend.at[CHUNKS + f], zrecv.at[CHUNKS + f], p.twin))
        c_wait(first + 1, gmrecv.at[f, 1])
        gzkeep[f] = gmsend[f, block(p.mine), :] + gmrecv[f, 1]

    stage_a(0)
    xf = x_ref[...].astype(F32)
    rstd_ref[...] = lax.rsqrt(jnp.mean(xf * xf, axis=1, keepdims=True) + 1e-06)
    keep = (ids_ref[...] != 0).astype(F32)
    keep_ref[...] = jnp.broadcast_to(keep, (tok, tok)).T[:, 0:1]
    igacc[...] = jnp.zeros_like(igacc)
    for k in range(NY):
        xt[:, k * tok:(k + 1) * tok] = xc[k].T
    loss = jnp.zeros((tok, 1), F32)
    for f in range(CHUNKS):
        if f + 1 < CHUNKS and f + 1 < EARLY:
            stage_a(f + 1)
        loss = loss + stage_b(f)
        if f + 1 < CHUNKS and f + 1 >= EARLY:
            if f >= 1:
                stage_c(f - 1)
            stage_a(f + 1)
        elif f >= 1:
            stage_c(f - 1)
    stage_c(CHUNKS - 1)
    loss_ref[...] = jnp.broadcast_to(loss * (0.5 / feat), (tok, tok)).T[0:1, :]

    last = 2 * CHUNKS
    for k in [2, 1, 3, 0]:
        igsend[k] = igacc[k * tok:(k + 1) * tok, :].astype(BF16)
        if k:
            back = NY - k
            go(remote(igsend.at[k], igrecv.at[y],
                      ysend.at[last, back], yrecv.at[last, back], p.at_y(back)))
    igrecv[y] = igsend[0]
    for k in range(1, NY):
        y_wait(last, k, igrecv.at[lax.rem(y - k + NY, NY)])
    rstd = rstd_ref[...]
    mean = jnp.zeros((tok, 1), F32)
    for q in range(NY):
        scaled = igrecv[q].astype(F32) * grow[q]
        xq = x_ref[:, q * chans:(q + 1) * chans].astype(F32)
        mean = mean + jnp.sum(scaled * xq, axis=1, keepdims=True)
    mean = mean * (rstd * (rstd / dim))
    for q in range(NY):
        scaled = igrecv[q].astype(F32) * grow[q]
        xq = x_ref[:, q * chans:(q + 1) * chans].astype(F32)
        gt_ref[:, q * chans:(q + 1) * chans] = (scaled - xq * mean).astype(BF16)

    scale = gcol[block(p.mine), 0:1] * (1.0 / (16.0 * tok) ** 0.5)
    for f in range(CHUNKS):
        z_wait(CHUNKS + f, gzrecv.at[f])
        gw_ref[:, cols[f]] = (gzkeep[f] + gzrecv[f].astype(F32)) * scale
    for copy in sent:
        copy.wait_send()


def step(x, ids, w, gain, xc, wfull, sfull, sg):
    tok, dim = x.shape
    rows, feat = w.shape
    chans = dim // NY
    width = feat // CHUNKS
    return pl.pallas_call(
        step_kernel,
        out_shape=(
            jax.ShapeDtypeStruct((rows, feat), F32),
            jax.ShapeDtypeStruct((tok, dim), BF16),
            jax.ShapeDtypeStruct((1, tok), F32),
        ),
        in_specs=[VM] * 8,
        out_specs=(VM,) * 3,
        scratch_shapes=[
            pltpu.VMEM((chans, NY * tok), BF16),
            pltpu.VMEM((max(CHUNKS - EARLY, 1), chans, width), BF16),
            pltpu.VMEM((chans, width), BF16),
            pltpu.VMEM((chans, 128), F32),
            pltpu.VMEM((chans, 128), F32),
            pltpu.VMEM((NY, 1, chans), F32),
            pltpu.VMEM((CHUNKS, tok, width), F32),
            pltpu.VMEM((CHUNKS, NY, tok, width), BF16),
            pltpu.VMEM((CHUNKS, NY, tok, width), BF16),
            pltpu.VMEM((CHUNKS, NY, tok, width), BF16),
            pltpu.VMEM((NY * tok, chans), F32),
            pltpu.VMEM((NY, tok, chans), BF16),
            pltpu.VMEM((NY, tok, chans), BF16),
            pltpu.VMEM((CHUNKS, chans, width), F32),
            pltpu.VMEM((CHUNKS, 2, rows, width), F32),
            pltpu.VMEM((CHUNKS, rows, width), F32),
            pltpu.VMEM((CHUNKS, rows, width), BF16),
            pltpu.VMEM((CHUNKS, rows, width), BF16),
            pltpu.VMEM((tok, 1), F32),
            pltpu.VMEM((tok, 1), F32),
            pltpu.SemaphoreType.DMA((1 + 2 * CHUNKS, NY)),
            pltpu.SemaphoreType.DMA((1 + 2 * CHUNKS, NY)),
            pltpu.SemaphoreType.DMA((3 * CHUNKS,)),
            pltpu.SemaphoreType.DMA((3 * CHUNKS,)),
            pltpu.SemaphoreType.DMA((2 * CHUNKS,)),
            pltpu.SemaphoreType.DMA((2 * CHUNKS,)),
        ],
        compiler_params=pltpu.CompilerParams(
            collective_id=0, has_side_effects=True, vmem_limit_bytes=40 * 2**20
        ),
        name="codistill_step",
    )(x, ids, w, gain, xc, wfull, sfull, sg)


def body(ngroups, tokens, token_ids, weight, stale_weight, gain, stale_gain, partner):
    branches = [functools.partial(exchange_for, m) for m in range(1, ngroups)]
    x, w = tokens[0], weight[0]
    xc, wfull, sfull, sg = lax.switch(
        partner[0] - 1, branches, x, w, stale_weight[0], stale_gain
    )
    gw, gt, loss = step(x, token_ids, w, gain, xc, wfull, sfull, sg)
    return gw[None], gt[None], loss


def solution(mesh):
    return jax.shard_map(
        functools.partial(body, mesh.shape["group"]),
        mesh=mesh,
        in_specs=(
            P("group", "fsdp", None),
            P("group", "fsdp"),
            P("group", "fsdp", None),
            P("group", "fsdp", None),
            P("group", None),
            P("group", None),
            P(),
        ),
        out_specs=(P("group", "fsdp", None), P("group", "fsdp", None), P("group", "fsdp")),
        check_vma=False,
    )
```

```python
import functools

import jax
import jax.numpy as jnp
from jax import lax
from jax.experimental import pallas as pl
from jax.experimental.pallas import tpu as pltpu
from jax.sharding import PartitionSpec as P

MESH = pl.DeviceIdType.MESH
NX = 4
NY = 4
CHUNKS = 4
UNROLL = True
AHEAD = 1
F32 = jnp.float32
BF16 = jnp.bfloat16
VM = pl.BlockSpec(memory_space=pltpu.VMEM)
SM = pl.BlockSpec(memory_space=pltpu.SMEM)


def flip_bits(index, m):
    bit = 1
    while bit <= m:
        if m & bit:
            index = index + bit * (1 - 2 * lax.rem(index // bit, 2))
        bit *= 2
    return index


def remote(src, dst, send, recv, dev):
    return pltpu.make_async_remote_copy(
        src_ref=src, dst_ref=dst, send_sem=send, recv_sem=recv,
        device_id=dev, device_id_type=MESH,
    )


def each(n, f, unroll=False):
    def go(i, carry):
        f(i)
        return carry

    lax.fori_loop(0, n, go, 0, unroll=unroll)


def rows16(i, base=0):
    return pl.ds(pl.multiple_of(base + i * 16, 16), 16)


def step_kernel(
    mz,
    partner_ref, x_ref, ids_ref, w_ref, s_ref, gain_ref, sgain_ref,
    gw_ref, gt_ref, loss_ref,
    x4, xc, xt, wfull, sfull, cfull, sx1, st1, sx2, st2,
    grow, sgrow, sgx, gcols,
    part, psend, precv, og, igacc, igsend, igrecv,
    gm, gmrecv, gzsend, gzrecv, rstd_ref, keep_ref, loss_acc,
    ysend, yrecv, csend, crecv, zsend, zrecv, xsend, xrecv,
):
    tok, dim = x_ref.shape
    rows, feat = w_ref.shape
    chans = dim // NY
    width = feat // CHUNKS
    grp = lax.axis_index("group")
    me = lax.axis_index("fsdp")
    y = me // 4
    mine = lax.rem(me, 4)
    zh = mine // 2
    core = lax.rem(mine, 2)
    far = (1 - zh) * 2 + core
    other = zh * 2 + (1 - core)
    otherfar = (1 - zh) * 2 + (1 - core)
    zpart = flip_bits(grp, mz * NX)
    mate = (grp, y * 4 + other)
    twin = (grp, y * 4 + far)
    near = (zpart, me)
    cross = (zpart, y * 4 + far)
    x1 = (flip_bits(grp, 1), me)
    x2 = (flip_bits(grp, 2), me)

    def at_y(k):
        return (grp, lax.rem(y + k, NY) * 4 + mine)

    def block(b):
        return pl.ds(pl.multiple_of(b * rows, 16), rows)

    def lanes(f):
        return pl.ds(pl.multiple_of(f * width, 128), width)

    IG, X = 2 * CHUNKS, 2 * CHUNKS + 1

    def y_copy(n, k, src, dst):
        return remote(src, dst, ysend.at[n, k], yrecv.at[n, k], at_y(k))

    def c_copy(n, f, src, dst):
        return remote(src, dst, csend.at[n, f], crecv.at[n, f], mate)

    def z_copy(n, f, src, dst, dev):
        return remote(src, dst, zsend.at[n, f], zrecv.at[n, f], dev)

    def x_copy(n, f, src, dst, dev):
        return remote(src, dst, xsend.at[n, f], xrecv.at[n, f], dev)

    def to_twin(f):
        z_copy(0, f, w_ref.at[:, lanes(f)], wfull.at[f, block(mine), :], twin).start()

    peers = [twin, mate, x1, x2] + [at_y(k) for k in range(1, NY)]
    if mz:
        peers += [near, cross]
    barrier = pltpu.get_barrier_semaphore()
    for peer in peers:
        pl.semaphore_signal(barrier, inc=1, device_id=peer, device_id_type=MESH)

    for q in range(NY):
        grow[q] = gain_ref[:, q * chans:(q + 1) * chans].astype(F32)
        sgrow[q] = sgain_ref[:, q * chans:(q + 1) * chans].astype(F32)

    def cut(i):
        at = rows16(i)
        xr = x_ref[at, :]
        for q in range(NY):
            x4[q, at, :] = xr[:, q * chans:(q + 1) * chans]
        xf = xr.astype(F32)
        rstd_ref[at, :] = lax.rsqrt(jnp.mean(xf * xf, axis=1, keepdims=True) + 1e-06)

    each(tok // 16, cut)
    pl.semaphore_wait(barrier, len(peers))

    x_copy(0, 0, sgrow.at[y], sgx.at[0], x1).start()

    def own(f):
        pl.when(f < AHEAD)(lambda: to_twin(f))
        x_copy(1, f, s_ref.at[:, lanes(f)], sx1.at[f], x1).start()
        c_copy(0, f, w_ref.at[:, lanes(f)], wfull.at[f, block(mine), :]).start()
        wfull[f, block(mine), :] = w_ref[:, lanes(f)]

    each(CHUNKS, own)

    def spread(k):
        y_copy(X, k, x4.at[lax.rem(y + k, NY)], xc.at[k]).start()

    each_k = lambda f: each(NY - 1, lambda i: f(i + 1))
    each_k(spread)
    xc[0] = x4[y]

    m = partner_ref[0]
    bit0 = lax.rem(m, 2) == 1
    bit1 = lax.rem(m // 2, 2) == 1
    x_copy(0, 0, sgrow.at[y], sgx.at[0], x1).wait_recv()
    sgx[1] = jnp.where(bit0, sgx[0], sgrow[y])
    x_copy(0, 1, sgx.at[1], sgx.at[2], x2).start()

    def first(f):
        x_copy(1, f, st1.at[f], sx1.at[f], x1).wait_recv()

        st1[f] = jnp.where(bit0, sx1[f], s_ref[:, lanes(f)])
        x_copy(2, f, st1.at[f], sx2.at[f], x2).start()

    each(CHUNKS, first)
    x_copy(0, 1, sgx.at[1], sgx.at[2], x2).wait_recv()
    sgx[3] = jnp.where(bit1, sgx[2], sgx[1])
    if mz:
        x_copy(0, 2, sgx.at[3], sgx.at[4], near).start()
    else:
        sgx[4] = sgx[3]

    def second(f):
        x_copy(2, f, st1.at[f], sx2.at[f], x2).wait_recv()

        st2[f] = jnp.where(bit1, sx2[f], st1[f])
        z_copy(2, f, st2.at[f], sfull.at[f, block(mine), :], cross).start()
        if mz:
            z_copy(1, f, st2.at[f], sfull.at[f, block(mine), :], near).start()
        else:
            sfull[f, block(mine), :] = st2[f]
        pl.when(f < CHUNKS - AHEAD)(lambda: to_twin(f + AHEAD))

    each(CHUNKS, second)

    keep = (ids_ref[...] != 0).astype(F32)
    keep_ref[...] = jnp.broadcast_to(keep, (tok, tok)).T[:, 0:1]
    loss_acc[...] = jnp.zeros_like(loss_acc)

    def clear(i):
        igacc[pl.ds(pl.multiple_of(i * tok, 128), tok), :] = jnp.zeros((tok, chans), F32)

    each(NY, clear)
    each_k(lambda k: y_copy(X, k, xc.at[k], xc.at[k]).wait_recv())

    def turn(k):
        xt[:, pl.ds(pl.multiple_of(k * tok, 128), tok)] = xc[k].T

    each(NY, turn)

    if mz:
        x_copy(0, 2, sgx.at[3], sgx.at[4], near).wait()
    sgx[3] = grow[y]

    def column(j):
        gcols[j] = jnp.broadcast_to(sgx[3 + j], (128, chans)).T

    each(2, column, UNROLL)

    def stage_a(f):
        z_copy(0, f, wfull.at[f, block(far), :], wfull.at[f, block(far), :], twin).wait_recv()
        c_copy(1, f, wfull.at[f, block(far), :], wfull.at[f, block(far), :]).start()
        if mz:
            z_copy(1, f, sfull.at[f, block(mine), :], sfull.at[f, block(mine), :], twin).wait_recv()
        z_copy(2, f, sfull.at[f, block(far), :], sfull.at[f, block(far), :], twin).wait_recv()

        def combine(n):
            b = mine + n * (far - mine)
            at = block(b)
            cfull[f, at, :] = (
                gcols[0, at, 0:1] * wfull[f, at, :].astype(F32)
                - gcols[1, at, 0:1] * sfull[f, at, :].astype(F32)
            ).astype(BF16)
            c_copy(2 + n, f, cfull.at[f, block(b), :], cfull.at[f, block(b), :]).start()

        each(2, combine)
        c_copy(0, f, wfull.at[f, block(other), :], wfull.at[f, block(other), :]).wait_recv()
        c_copy(1, f, wfull.at[f, block(otherfar), :], wfull.at[f, block(otherfar), :]).wait_recv()
        c_copy(2, f, cfull.at[f, block(other), :], cfull.at[f, block(other), :]).wait_recv()
        c_copy(3, f, cfull.at[f, block(otherfar), :], cfull.at[f, block(otherfar), :]).wait_recv()

        def product(i):
            k = lax.rem(i + 1, NY)
            got = jnp.dot(xc[k], cfull[f], preferred_element_type=F32)
            part[f, k] = got
            psend[f, k] = got.astype(BF16)

            @pl.when(i < NY - 1)
            def _():
                y_copy(f, NY - k, psend.at[f, k], precv.at[f, NY - k]).start()

        each(NY, product, UNROLL)

    def stage_b(f):
        each_k(lambda k: y_copy(f, k, precv.at[f, k], precv.at[f, k]).wait_recv())

        total = part[f, 0]
        for k in range(1, NY):
            total = total + precv[f, k].astype(F32)
        rstd = rstd_ref[...]
        diff = total * (rstd * keep_ref[...])
        og[f, 0] = (diff * rstd).astype(BF16)
        loss_acc[...] += jnp.sum(diff * diff, axis=1, keepdims=True)
        each_k(lambda k: y_copy(CHUNKS + f, k, og.at[f, 0], og.at[f, k]).start())

    def stage_c(f):
        each_k(lambda k: y_copy(CHUNKS + f, k, og.at[f, k], og.at[f, k]).wait_recv())

        def outer(j):
            b = ((1 - zh) + lax.rem(j, 2) * (2 * zh - 1)) * 2 + (1 - core) + (j // 2) * (2 * core - 1)
            gm[f, block(b), :] = jnp.dot(
                xt[block(b), :], og[f].reshape(NY * tok, width), preferred_element_type=F32
            )

            @pl.when(j < 2)
            def _():
                c_copy(4 + j, f, gm.at[f, block(b), :], gmrecv.at[f, j]).start()

        each(NY, outer, UNROLL)

        def back(k):
            at = pl.ds(pl.multiple_of(k * tok, 128), tok)
            igacc[at, :] += lax.dot_general(
                og[f, k], wfull[f], (((1,), (1,)), ((), ())), preferred_element_type=F32
            )

        each(NY, back, UNROLL)
        c_copy(4, f, gmrecv.at[f, 0], gmrecv.at[f, 0]).wait_recv()

        gzsend[f] = (gm[f, block(far), :] + gmrecv[f, 0]).astype(BF16)
        z_copy(3, f, gzsend.at[f], gzrecv.at[f], twin).start()
        c_copy(5, f, gmrecv.at[f, 1], gmrecv.at[f, 1]).wait_recv()

    def turnover(t):
        pl.when(t < CHUNKS)(lambda: stage_a(t))
        pl.when((t >= 1) & (t <= CHUNKS))(lambda: stage_b(t - 1))
        pl.when(t >= 2)(lambda: stage_c(t - 2))

    each(CHUNKS + 2, turnover)
    loss_ref[...] = jnp.broadcast_to(loss_acc[...] * (0.5 / feat), (tok, tok)).T[0:1, :]

    def home(i):
        k = lax.rem(i + 1, NY)
        at = pl.ds(pl.multiple_of(k * tok, 128), tok)
        igsend[k] = igacc[at, :].astype(BF16)

        @pl.when(i < NY - 1)
        def _():
            y_copy(IG, NY - k, igsend.at[k], igrecv.at[y]).start()

    each(NY, home)
    igrecv[y] = igsend[0]
    each_k(lambda k: y_copy(IG, k, igrecv.at[lax.rem(y - k + NY, NY)], igrecv.at[lax.rem(y - k + NY, NY)]).wait_recv())

    def tokens_back(i):
        at = rows16(i)
        rstd = rstd_ref[at, :]
        scaled = [igrecv[q, at, :].astype(F32) * grow[q] for q in range(NY)]
        xq = [x4[q, at, :].astype(F32) for q in range(NY)]
        mean = sum(jnp.sum(s * v, axis=1, keepdims=True) for s, v in zip(scaled, xq))
        mean = mean * (rstd * (rstd / dim))
        for q in range(NY):
            gt_ref[at, q * chans:(q + 1) * chans] = (scaled[q] - xq[q] * mean).astype(BF16)

    each(tok // 16, tokens_back)

    def finish(f):
        z_copy(3, f, gzrecv.at[f], gzrecv.at[f], twin).wait_recv()

        scale = gcols[0, block(mine), 0:1] * (1.0 / (16.0 * tok) ** 0.5)
        total = gm[f, block(mine), :] + gmrecv[f, 1] + gzrecv[f].astype(F32)
        gw_ref[:, lanes(f)] = total * scale

    each(CHUNKS, finish)

    x_copy(0, 0, sgrow.at[y], sgx.at[0], x1).wait_send()
    x_copy(0, 1, sgx.at[1], sgx.at[2], x2).wait_send()

    def left(f):
        for n in [0, 1, 2, 3] if mz else [0, 2, 3]:
            z_copy(n, f, gzsend.at[f], gzsend.at[f], twin).wait_send()
        for n in (1, 2):
            x_copy(n, f, st1.at[f], sx1.at[f], x1).wait_send()
        for n in range(4):
            c_copy(n, f, gzsend.at[f], gzsend.at[f]).wait_send()
        for n in range(2):
            c_copy(4 + n, f, gmrecv.at[f, n], gmrecv.at[f, n]).wait_send()

    each(CHUNKS, left)

    def left_y(k):
        each(2 * CHUNKS, lambda n: y_copy(n, k, og.at[0, 0], og.at[0, 0]).wait_send())
        for n in (IG, X):
            y_copy(n, k, igsend.at[0], igsend.at[0]).wait_send()

    each_k(left_y)


def step_for(mz, x, ids, w, s, gain, sgain, partner):
    tok, dim = x.shape
    rows, feat = w.shape
    chans = dim // NY
    width = feat // CHUNKS
    return pl.pallas_call(
        functools.partial(step_kernel, mz),
        out_shape=(
            jax.ShapeDtypeStruct((rows, feat), F32),
            jax.ShapeDtypeStruct((tok, dim), BF16),
            jax.ShapeDtypeStruct((1, tok), F32),
        ),
        in_specs=[SM] + [VM] * 6,
        out_specs=(VM,) * 3,
        scratch_shapes=[
            pltpu.VMEM((NY, tok, chans), BF16),
            pltpu.VMEM((NY, tok, chans), BF16),
            pltpu.VMEM((chans, NY * tok), BF16),
            pltpu.VMEM((CHUNKS, chans, width), BF16),
            pltpu.VMEM((CHUNKS, chans, width), BF16),
            pltpu.VMEM((CHUNKS, chans, width), BF16),
            pltpu.VMEM((CHUNKS, rows, width), BF16),
            pltpu.VMEM((CHUNKS, rows, width), BF16),
            pltpu.VMEM((CHUNKS, rows, width), BF16),
            pltpu.VMEM((CHUNKS, rows, width), BF16),
            pltpu.VMEM((NY, 1, chans), F32),
            pltpu.VMEM((NY, 1, chans), F32),
            pltpu.VMEM((5, 1, chans), F32),
            pltpu.VMEM((2, chans, 128), F32),
            pltpu.VMEM((CHUNKS, NY, tok, width), F32),
            pltpu.VMEM((CHUNKS, NY, tok, width), BF16),
            pltpu.VMEM((CHUNKS, NY, tok, width), BF16),
            pltpu.VMEM((CHUNKS, NY, tok, width), BF16),
            pltpu.VMEM((NY * tok, chans), F32),
            pltpu.VMEM((NY, tok, chans), BF16),
            pltpu.VMEM((NY, tok, chans), BF16),
            pltpu.VMEM((CHUNKS, chans, width), F32),
            pltpu.VMEM((CHUNKS, 2, rows, width), F32),
            pltpu.VMEM((CHUNKS, rows, width), BF16),
            pltpu.VMEM((CHUNKS, rows, width), BF16),
            pltpu.VMEM((tok, 1), F32),
            pltpu.VMEM((tok, 1), F32),
            pltpu.VMEM((tok, 1), F32),
            pltpu.SemaphoreType.DMA((2 + 2 * CHUNKS, NY)),
            pltpu.SemaphoreType.DMA((2 + 2 * CHUNKS, NY)),
            pltpu.SemaphoreType.DMA((6, CHUNKS)),
            pltpu.SemaphoreType.DMA((6, CHUNKS)),
            pltpu.SemaphoreType.DMA((4, CHUNKS)),
            pltpu.SemaphoreType.DMA((4, CHUNKS)),
            pltpu.SemaphoreType.DMA((3, max(CHUNKS, 3))),
            pltpu.SemaphoreType.DMA((3, max(CHUNKS, 3))),
        ],
        compiler_params=pltpu.CompilerParams(
            collective_id=mz, has_side_effects=True, vmem_limit_bytes=48 * 2**20
        ),
        name="codistill_step",
    )(partner, x, ids, w, s, gain, sgain)


def body(ngroups, tokens, token_ids, weight, stale_weight, gain, stale_gain, partner):
    branches = [functools.partial(step_for, mz) for mz in range(ngroups // NX)]
    gw, gt, loss = lax.switch(
        partner[0] // NX, branches,
        tokens[0], token_ids, weight[0], stale_weight[0], gain, stale_gain, partner,
    )
    return gw[None], gt[None], loss


def solution(mesh):
    return jax.shard_map(
        functools.partial(body, mesh.shape["group"]),
        mesh=mesh,
        in_specs=(
            P("group", "fsdp", None),
            P("group", "fsdp"),
            P("group", "fsdp", None),
            P("group", "fsdp", None),
            P("group", None),
            P("group", None),
            P(),
        ),
        out_specs=(P("group", "fsdp", None), P("group", "fsdp", None), P("group", "fsdp")),
        check_vma=False,
    )
```

```python
import functools

import jax
import jax.numpy as jnp
from jax import lax
from jax.experimental import pallas as pl
from jax.experimental.pallas import tpu as pltpu
from jax.sharding import PartitionSpec as P

MESH = pl.DeviceIdType.MESH
NX = 4
NY = 4
CHUNKS = 4
UNROLL = False
AHEAD = 1
F32 = jnp.float32
BF16 = jnp.bfloat16
VM = pl.BlockSpec(memory_space=pltpu.VMEM)
SM = pl.BlockSpec(memory_space=pltpu.SMEM)


def flip_bits(index, m):
    bit = 1
    while bit <= m:
        if m & bit:
            index = index + bit * (1 - 2 * lax.rem(index // bit, 2))
        bit *= 2
    return index


def remote(src, dst, send, recv, dev):
    return pltpu.make_async_remote_copy(
        src_ref=src, dst_ref=dst, send_sem=send, recv_sem=recv,
        device_id=dev, device_id_type=MESH,
    )


def each(n, f, unroll=False):
    def go(i, carry):
        f(i)
        return carry

    lax.fori_loop(0, n, go, 0, unroll=unroll)


def rows16(i, base=0):
    return pl.ds(pl.multiple_of(base + i * 16, 16), 16)


def step_kernel(
    mz,
    partner_ref, x_ref, ids_ref, w_ref, s_ref, gain_ref, sgain_ref,
    gw_ref, gt_ref, loss_ref,
    x4, xc, xt, wfull, sfull, cfull, sx1, st1, sx2, st2,
    grow, sgrow, sgx, gcols,
    part, psend, precv, og, igacc, igsend, igrecv,
    gm, gmrecv, gzsend, gzrecv, rstd_ref, keep_ref, loss_acc,
    ysend, yrecv, csend, crecv, zsend, zrecv, xsend, xrecv,
):
    tok, dim = x_ref.shape
    rows, feat = w_ref.shape
    chans = dim // NY
    width = feat // CHUNKS
    grp = lax.axis_index("group")
    me = lax.axis_index("fsdp")
    y = me // 4
    mine = lax.rem(me, 4)
    zh = mine // 2
    core = lax.rem(mine, 2)
    far = (1 - zh) * 2 + core
    other = zh * 2 + (1 - core)
    otherfar = (1 - zh) * 2 + (1 - core)
    zpart = flip_bits(grp, mz * NX)
    mate = (grp, y * 4 + other)
    twin = (grp, y * 4 + far)
    near = (zpart, me)
    cross = (zpart, y * 4 + far)
    x1 = (flip_bits(grp, 1), me)
    x2 = (flip_bits(grp, 2), me)

    def at_y(k):
        return (grp, lax.rem(y + k, NY) * 4 + mine)

    def block(b):
        return pl.ds(pl.multiple_of(b * rows, 16), rows)

    def lanes(f):
        return pl.ds(pl.multiple_of(f * width, 128), width)

    IG, X = 2 * CHUNKS, 2 * CHUNKS + 1

    def y_copy(n, k, src, dst):
        return remote(src, dst, ysend.at[n, k], yrecv.at[n, k], at_y(k))

    def c_copy(n, f, src, dst):
        return remote(src, dst, csend.at[n, f], crecv.at[n, f], mate)

    def z_copy(n, f, src, dst, dev):
        return remote(src, dst, zsend.at[n, f], zrecv.at[n, f], dev)

    def x_copy(n, f, src, dst, dev):
        return remote(src, dst, xsend.at[n, f], xrecv.at[n, f], dev)

    def to_twin(f):
        z_copy(0, f, w_ref.at[:, lanes(f)], wfull.at[f, block(mine), :], twin).start()

    peers = [twin, mate, x1, x2] + [at_y(k) for k in range(1, NY)]
    if mz:
        peers += [near, cross]
    barrier = pltpu.get_barrier_semaphore()
    for peer in peers:
        pl.semaphore_signal(barrier, inc=1, device_id=peer, device_id_type=MESH)

    for q in range(NY):
        grow[q] = gain_ref[:, q * chans:(q + 1) * chans].astype(F32)
        sgrow[q] = sgain_ref[:, q * chans:(q + 1) * chans].astype(F32)

    def cut(i):
        at = rows16(i)
        xr = x_ref[at, :]
        for q in range(NY):
            x4[q, at, :] = xr[:, q * chans:(q + 1) * chans]
        xf = xr.astype(F32)
        rstd_ref[at, :] = lax.rsqrt(jnp.mean(xf * xf, axis=1, keepdims=True) + 1e-06)

    each(tok // 16, cut)
    pl.semaphore_wait(barrier, len(peers))

    x_copy(0, 0, sgrow.at[y], sgx.at[0], x1).start()

    def own(f):
        pl.when(f < AHEAD)(lambda: to_twin(f))
        x_copy(1, f, s_ref.at[:, lanes(f)], sx1.at[f], x1).start()
        c_copy(0, f, w_ref.at[:, lanes(f)], wfull.at[f, block(mine), :]).start()
        wfull[f, block(mine), :] = w_ref[:, lanes(f)]

    each(CHUNKS, own)

    def spread(k):
        y_copy(X, k, x4.at[lax.rem(y + k, NY)], xc.at[k]).start()

    each_k = lambda f: each(NY - 1, lambda i: f(i + 1))
    each_k(spread)
    xc[0] = x4[y]

    m = partner_ref[0]
    bit0 = lax.rem(m, 2) == 1
    bit1 = lax.rem(m // 2, 2) == 1
    x_copy(0, 0, sgrow.at[y], sgx.at[0], x1).wait_recv()
    sgx[1] = jnp.where(bit0, sgx[0], sgrow[y])
    x_copy(0, 1, sgx.at[1], sgx.at[2], x2).start()

    def first(f):
        x_copy(1, f, st1.at[f], sx1.at[f], x1).wait_recv()

        st1[f] = jnp.where(bit0, sx1[f], s_ref[:, lanes(f)])
        x_copy(2, f, st1.at[f], sx2.at[f], x2).start()

    each(CHUNKS, first)
    x_copy(0, 1, sgx.at[1], sgx.at[2], x2).wait_recv()
    sgx[3] = jnp.where(bit1, sgx[2], sgx[1])
    if mz:
        x_copy(0, 2, sgx.at[3], sgx.at[4], near).start()
    else:
        sgx[4] = sgx[3]

    def second(f):
        x_copy(2, f, st1.at[f], sx2.at[f], x2).wait_recv()

        st2[f] = jnp.where(bit1, sx2[f], st1[f])
        z_copy(2, f, st2.at[f], sfull.at[f, block(mine), :], cross).start()
        if mz:
            z_copy(1, f, st2.at[f], sfull.at[f, block(mine), :], near).start()
        else:
            sfull[f, block(mine), :] = st2[f]
        pl.when(f < CHUNKS - AHEAD)(lambda: to_twin(f + AHEAD))

    each(CHUNKS, second)

    keep = (ids_ref[...] != 0).astype(F32)
    keep_ref[...] = jnp.broadcast_to(keep, (tok, tok)).T[:, 0:1]
    loss_acc[...] = jnp.zeros_like(loss_acc)

    def clear(i):
        igacc[pl.ds(pl.multiple_of(i * tok, 128), tok), :] = jnp.zeros((tok, chans), F32)

    each(NY, clear)
    each_k(lambda k: y_copy(X, k, xc.at[k], xc.at[k]).wait_recv())

    def turn(k):
        xt[:, pl.ds(pl.multiple_of(k * tok, 128), tok)] = xc[k].T

    each(NY, turn)

    if mz:
        x_copy(0, 2, sgx.at[3], sgx.at[4], near).wait()
    sgx[3] = grow[y]

    def column(j):
        gcols[j] = jnp.broadcast_to(sgx[3 + j], (128, chans)).T

    each(2, column)

    def stage_a(f):
        z_copy(0, f, wfull.at[f, block(far), :], wfull.at[f, block(far), :], twin).wait_recv()
        c_copy(1, f, wfull.at[f, block(far), :], wfull.at[f, block(far), :]).start()
        if mz:
            z_copy(1, f, sfull.at[f, block(mine), :], sfull.at[f, block(mine), :], twin).wait_recv()
        z_copy(2, f, sfull.at[f, block(far), :], sfull.at[f, block(far), :], twin).wait_recv()

        def combine(n):
            b = mine + n * (far - mine)
            at = block(b)
            cfull[f, at, :] = (
                gcols[0, at, 0:1] * wfull[f, at, :].astype(F32)
                - gcols[1, at, 0:1] * sfull[f, at, :].astype(F32)
            ).astype(BF16)
            c_copy(2 + n, f, cfull.at[f, block(b), :], cfull.at[f, block(b), :]).start()

        each(2, combine)
        c_copy(0, f, wfull.at[f, block(other), :], wfull.at[f, block(other), :]).wait_recv()
        c_copy(1, f, wfull.at[f, block(otherfar), :], wfull.at[f, block(otherfar), :]).wait_recv()
        c_copy(2, f, cfull.at[f, block(other), :], cfull.at[f, block(other), :]).wait_recv()
        c_copy(3, f, cfull.at[f, block(otherfar), :], cfull.at[f, block(otherfar), :]).wait_recv()

        def product(i):
            k = lax.rem(i + 1, NY)
            got = jnp.dot(xc[k], cfull[f], preferred_element_type=F32)
            part[f, k] = got
            psend[f, k] = got.astype(BF16)

            @pl.when(i < NY - 1)
            def _():
                y_copy(f, NY - k, psend.at[f, k], precv.at[f, NY - k]).start()

        each(NY, product, UNROLL)

    def stage_b(f):
        each_k(lambda k: y_copy(f, k, precv.at[f, k], precv.at[f, k]).wait_recv())

        total = part[f, 0]
        for k in range(1, NY):
            total = total + precv[f, k].astype(F32)
        rstd = rstd_ref[...]
        diff = total * (rstd * keep_ref[...])
        og[f, 0] = (diff * rstd).astype(BF16)
        loss_acc[...] += jnp.sum(diff * diff, axis=1, keepdims=True)
        each_k(lambda k: y_copy(CHUNKS + f, k, og.at[f, 0], og.at[f, k]).start())

    def stage_c(f):
        each_k(lambda k: y_copy(CHUNKS + f, k, og.at[f, k], og.at[f, k]).wait_recv())

        def outer(j):
            b = ((1 - zh) + lax.rem(j, 2) * (2 * zh - 1)) * 2 + (1 - core) + (j // 2) * (2 * core - 1)
            gm[f, block(b), :] = jnp.dot(
                xt[block(b), :], og[f].reshape(NY * tok, width), preferred_element_type=F32
            )

            @pl.when(j < 2)
            def _():
                c_copy(4 + j, f, gm.at[f, block(b), :], gmrecv.at[f, j]).start()

        each(NY, outer, UNROLL)

        def back(k):
            at = pl.ds(pl.multiple_of(k * tok, 128), tok)
            igacc[at, :] += lax.dot_general(
                og[f, k], wfull[f], (((1,), (1,)), ((), ())), preferred_element_type=F32
            )

        each(NY, back, UNROLL)
        c_copy(4, f, gmrecv.at[f, 0], gmrecv.at[f, 0]).wait_recv()

        gzsend[f] = (gm[f, block(far), :] + gmrecv[f, 0]).astype(BF16)
        z_copy(3, f, gzsend.at[f], gzrecv.at[f], twin).start()
        c_copy(5, f, gmrecv.at[f, 1], gmrecv.at[f, 1]).wait_recv()

    def turnover(t):
        pl.when(t < CHUNKS)(lambda: stage_a(t))
        pl.when((t >= 1) & (t <= CHUNKS))(lambda: stage_b(t - 1))
        pl.when(t >= 2)(lambda: stage_c(t - 2))

    each(CHUNKS + 2, turnover)
    loss_ref[...] = jnp.broadcast_to(loss_acc[...] * (0.5 / feat), (tok, tok)).T[0:1, :]

    def home(i):
        k = lax.rem(i + 1, NY)
        at = pl.ds(pl.multiple_of(k * tok, 128), tok)
        igsend[k] = igacc[at, :].astype(BF16)

        @pl.when(i < NY - 1)
        def _():
            y_copy(IG, NY - k, igsend.at[k], igrecv.at[y]).start()

    each(NY, home)
    igrecv[y] = igsend[0]
    each_k(lambda k: y_copy(IG, k, igrecv.at[lax.rem(y - k + NY, NY)], igrecv.at[lax.rem(y - k + NY, NY)]).wait_recv())

    def tokens_back(i):
        at = rows16(i)
        rstd = rstd_ref[at, :]
        scaled = [igrecv[q, at, :].astype(F32) * grow[q] for q in range(NY)]
        xq = [x4[q, at, :].astype(F32) for q in range(NY)]
        mean = sum(jnp.sum(s * v, axis=1, keepdims=True) for s, v in zip(scaled, xq))
        mean = mean * (rstd * (rstd / dim))
        for q in range(NY):
            gt_ref[at, q * chans:(q + 1) * chans] = (scaled[q] - xq[q] * mean).astype(BF16)

    each(tok // 16, tokens_back)

    def finish(f):
        z_copy(3, f, gzrecv.at[f], gzrecv.at[f], twin).wait_recv()

        scale = gcols[0, block(mine), 0:1] * (1.0 / (16.0 * tok) ** 0.5)
        total = gm[f, block(mine), :] + gmrecv[f, 1] + gzrecv[f].astype(F32)
        gw_ref[:, lanes(f)] = total * scale

    each(CHUNKS, finish)

    x_copy(0, 0, sgrow.at[y], sgx.at[0], x1).wait_send()
    x_copy(0, 1, sgx.at[1], sgx.at[2], x2).wait_send()

    def left(f):
        for n in [0, 1, 2, 3] if mz else [0, 2, 3]:
            z_copy(n, f, gzsend.at[f], gzsend.at[f], twin).wait_send()
        for n in (1, 2):
            x_copy(n, f, st1.at[f], sx1.at[f], x1).wait_send()
        for n in range(4):
            c_copy(n, f, gzsend.at[f], gzsend.at[f]).wait_send()
        for n in range(2):
            c_copy(4 + n, f, gmrecv.at[f, n], gmrecv.at[f, n]).wait_send()

    each(CHUNKS, left)

    def left_y(k):
        each(2 * CHUNKS, lambda n: y_copy(n, k, og.at[0, 0], og.at[0, 0]).wait_send())
        for n in (IG, X):
            y_copy(n, k, igsend.at[0], igsend.at[0]).wait_send()

    each_k(left_y)


def step_for(mz, x, ids, w, s, gain, sgain, partner):
    tok, dim = x.shape
    rows, feat = w.shape
    chans = dim // NY
    width = feat // CHUNKS
    return pl.pallas_call(
        functools.partial(step_kernel, mz),
        out_shape=(
            jax.ShapeDtypeStruct((rows, feat), F32),
            jax.ShapeDtypeStruct((tok, dim), BF16),
            jax.ShapeDtypeStruct((1, tok), F32),
        ),
        in_specs=[SM] + [VM] * 6,
        out_specs=(VM,) * 3,
        scratch_shapes=[
            pltpu.VMEM((NY, tok, chans), BF16),
            pltpu.VMEM((NY, tok, chans), BF16),
            pltpu.VMEM((chans, NY * tok), BF16),
            pltpu.VMEM((CHUNKS, chans, width), BF16),
            pltpu.VMEM((CHUNKS, chans, width), BF16),
            pltpu.VMEM((CHUNKS, chans, width), BF16),
            pltpu.VMEM((CHUNKS, rows, width), BF16),
            pltpu.VMEM((CHUNKS, rows, width), BF16),
            pltpu.VMEM((CHUNKS, rows, width), BF16),
            pltpu.VMEM((CHUNKS, rows, width), BF16),
            pltpu.VMEM((NY, 1, chans), F32),
            pltpu.VMEM((NY, 1, chans), F32),
            pltpu.VMEM((5, 1, chans), F32),
            pltpu.VMEM((2, chans, 128), F32),
            pltpu.VMEM((CHUNKS, NY, tok, width), F32),
            pltpu.VMEM((CHUNKS, NY, tok, width), BF16),
            pltpu.VMEM((CHUNKS, NY, tok, width), BF16),
            pltpu.VMEM((CHUNKS, NY, tok, width), BF16),
            pltpu.VMEM((NY * tok, chans), F32),
            pltpu.VMEM((NY, tok, chans), BF16),
            pltpu.VMEM((NY, tok, chans), BF16),
            pltpu.VMEM((CHUNKS, chans, width), F32),
            pltpu.VMEM((CHUNKS, 2, rows, width), F32),
            pltpu.VMEM((CHUNKS, rows, width), BF16),
            pltpu.VMEM((CHUNKS, rows, width), BF16),
            pltpu.VMEM((tok, 1), F32),
            pltpu.VMEM((tok, 1), F32),
            pltpu.VMEM((tok, 1), F32),
            pltpu.SemaphoreType.DMA((2 + 2 * CHUNKS, NY)),
            pltpu.SemaphoreType.DMA((2 + 2 * CHUNKS, NY)),
            pltpu.SemaphoreType.DMA((6, CHUNKS)),
            pltpu.SemaphoreType.DMA((6, CHUNKS)),
            pltpu.SemaphoreType.DMA((4, CHUNKS)),
            pltpu.SemaphoreType.DMA((4, CHUNKS)),
            pltpu.SemaphoreType.DMA((3, max(CHUNKS, 3))),
            pltpu.SemaphoreType.DMA((3, max(CHUNKS, 3))),
        ],
        compiler_params=pltpu.CompilerParams(
            collective_id=mz, has_side_effects=True, vmem_limit_bytes=48 * 2**20
        ),
        name="codistill_step",
    )(partner, x, ids, w, s, gain, sgain)


def body(ngroups, tokens, token_ids, weight, stale_weight, gain, stale_gain, partner):
    branches = [functools.partial(step_for, mz) for mz in range(ngroups // NX)]
    gw, gt, loss = lax.switch(
        partner[0] // NX, branches,
        tokens[0], token_ids, weight[0], stale_weight[0], gain, stale_gain, partner,
    )
    return gw[None], gt[None], loss


def solution(mesh):
    return jax.shard_map(
        functools.partial(body, mesh.shape["group"]),
        mesh=mesh,
        in_specs=(
            P("group", "fsdp", None),
            P("group", "fsdp"),
            P("group", "fsdp", None),
            P("group", "fsdp", None),
            P("group", None),
            P("group", None),
            P(),
        ),
        out_specs=(P("group", "fsdp", None), P("group", "fsdp", None), P("group", "fsdp")),
        check_vma=False,
    )
```
